32 devices in a mesh: groups: 2 (over y), row: 8 (over z, x), col: 2 (over core).
Axes of the slice: x: 2, y: 2, z: 4, core: 2. Of those that a mesh axis runs over, the one named last changes fastest.
Arguments:
- sigma_anc: bfloat16 [16384, 8192], P(('groups', 'row'), 'col'), parts along dimension 0, as said below
- panel: bfloat16 [16384, 3072], P(('groups', 'row'), 'col'), parts along dimension 0
- holder: int32 [128], P('groups'), parts along dimension 0, may hold values from 0 to 63, each once
- dinv_diag: float32 [6144], P(('groups', 'col')), parts along dimension 0, may hold values from 0.5 to 2
Outputs:
- sigma_aj: bfloat16 [16384, 3072], P(('groups', 'row'), 'col'), parts along dimension 0
- variances: float32 [6144], P(('groups', 'col')), parts along dimension 0
The draws below stay inside these ranges and needn't reach their ends.
There are 2 independent parts, one for each index of `groups`. The reference program is written for one: setup_inputs(seed, part) draws one part's arguments, and reference() takes and returns one part's arrays. A program takes and returns all parts, laid end to end along the dimension named above; each array names one. Nothing has to cross between parts.
Inputs may be any that keep to these rules, and one draw needn't show every extreme that they name: holder is a permutation of the 64 tiles. sigma_anc is symmetric and positive definite.
All inputs are finite; a program needn't handle non-finite values.
Results may differ from the reference program's by a relative error of at most 0.001.
Values may be sent and summed in bfloat16 or wider, within the bound.
No kernel may reach another device: no remote copies, remote signals or barrier semaphores. Data moves between devices by JAX's collectives and lax.ppermute only.
A program may use at most 128 MiB of HBM per device.

```python
import math
import jax
import jax.numpy as jnp

A = 8192
S = 3072
TILE = 128
TILES = 64


def draw_sigma_anc(key, part):
    kone = jax.random.fold_in(key, 11)
    ktwo = jax.random.fold_in(key, 12)
    base = jax.random.normal(kone, (A, A), jnp.float32)
    sym = (base + base.T) * (0.5 / jnp.sqrt(jnp.float32(A)))
    diag = jax.random.uniform(ktwo, (A,), jnp.float32, 1.5, 3.0)
    return (sym + jnp.diag(diag)).astype(jnp.bfloat16)


def draw_panel(key, part):
    kone = jax.random.fold_in(key, 21)
    ktwo = jax.random.fold_in(key, 22)
    rows = jnp.arange(A, dtype=jnp.float32) / A
    row_scale = 10.0 ** (rows - 0.5)
    col_scale = 10.0 ** jax.random.uniform(ktwo, (S,), jnp.float32, -0.5, 0.5)
    entries = jax.random.normal(kone, (A, S), jnp.float32)
    vals = entries * row_scale[:, None] * col_scale[None, :] / jnp.sqrt(jnp.float32(A))
    return vals.astype(jnp.bfloat16)


def block_levels(stream_key, shape, split, least, largest):
    def one(position, parts):
        heights = jax.random.uniform(jax.random.fold_in(jax.random.fold_in(stream_key, 6), position), (parts,), jnp.float32, least / len(split), largest / len(split))
        return jnp.repeat(jnp.exp(heights), shape[position] // parts).reshape((-1,) + (1,) * (len(shape) - position - 1))

    loudness = one(*split[0])
    for cut in split[1:]:
        loudness = loudness * one(*cut)
    return loudness


def setup_inputs(seed: int = 0, part: int = 0) -> dict:
    key_of = jax.random.split(jax.random.key(seed), 5)
    part_keys = jax.random.split(jax.random.fold_in(key_of[4], part), 5)
    return {
        "sigma_anc": draw_sigma_anc(jax.random.fold_in(jax.random.fold_in(key_of[4], part), 71), part),
        "panel": draw_panel(jax.random.fold_in(jax.random.fold_in(key_of[4], part), 71), part),
        "holder": jax.random.permutation(part_keys[2], TILES).astype(jnp.int32),
        "dinv_diag": jnp.clip(jnp.exp(math.log(2.0) - 1.3862944 * jax.random.uniform(part_keys[3], (S,), jnp.float32) ** block_levels(part_keys[3], (S,), ((0, 2),), -0.2, 0.2)), 0.5, 2.0),
    }


def reference(sigma_anc, panel, holder, dinv_diag):
    tiles = panel.reshape(TILES, TILE, S)
    panel_log = jnp.take(tiles, holder.astype(jnp.int32), axis=0).reshape(A, S)
    prod = jnp.dot(sigma_anc, panel_log, preferred_element_type=jnp.float32)
    sigma_aj = (-prod).astype(jnp.bfloat16)
    variances = dinv_diag + jnp.sum(panel_log.astype(jnp.float32) * prod, axis=0)
    return sigma_aj, variances
```

```python
import functools

import jax
import jax.numpy as jnp
from jax import lax
from jax.experimental import pallas as pl
from jax.experimental.pallas import tpu as pltpu
from jax.sharding import PartitionSpec as P

TILE = 128
F32 = jnp.float32
VMEM_LIMIT = 56 * 1024 * 1024


def reorder_kernel(slots, a, o):
    o[...] = a[...]


def reorder(whole, logical):
    rows, width = whole.shape
    return pl.pallas_call(
        reorder_kernel,
        grid_spec=pltpu.PrefetchScalarGridSpec(
            num_scalar_prefetch=1,
            grid=(width // TILE,),
            in_specs=[pl.BlockSpec((rows, TILE), lambda k, t: (0, t[k]))],
            out_specs=pl.BlockSpec((rows, TILE), lambda k, t: (0, k)),
        ),
        out_shape=jax.ShapeDtypeStruct((rows, width), whole.dtype),
        cost_estimate=pl.CostEstimate(flops=0, bytes_accessed=4 * rows * width, transcendentals=0),
    )(logical, whole)


def pick_kernel(count, here, at, *refs):
    j = pl.program_id(0)
    pieces, base, out = refs[:count], refs[count], refs[count + 1]
    value = base[...]
    for p in range(count):
        value = jnp.where(here[p, j] != 0, pieces[p][...], value)
    out[...] = value


def pick(pieces, sources, wanted, base):
    rows, cols = base.shape
    per = rows // TILE
    rel = jnp.stack([wanted - s * per for s in sources])
    here = ((rel >= 0) & (rel < per)).astype(jnp.int32)
    at = jnp.clip(rel, 0, per - 1)
    count = len(pieces)
    specs = [
        pl.BlockSpec((TILE, cols), functools.partial(lambda p, j, h, a: (a[p, j], 0), p))
        for p in range(count)
    ]
    tile = pl.BlockSpec((TILE, cols), lambda j, h, a: (j, 0))
    return pl.pallas_call(
        functools.partial(pick_kernel, count),
        grid_spec=pltpu.PrefetchScalarGridSpec(
            num_scalar_prefetch=2,
            grid=(per,),
            in_specs=specs + [tile],
            out_specs=tile,
        ),
        out_shape=jax.ShapeDtypeStruct((rows, cols), base.dtype),
        cost_estimate=pl.CostEstimate(
            flops=0, bytes_accessed=2 * (count + 2) * rows * cols, transcendentals=0
        ),
    )(here, at, *pieces, base)


def finish_kernel(tiles, here, at, acc, coeff, left, right, mine, out, part):
    i = pl.program_id(0)

    @pl.when(i == 0)
    def _():
        part[...] = jnp.zeros_like(part)

    half = left.shape[1]
    for late, lo in ((left, 0), (right, half)):
        span = pl.ds(lo, half)
        prod = acc[:, span] + jnp.dot(coeff[...], late[...], preferred_element_type=F32)
        out[:, span] = (-prod).astype(out.dtype)
        for t in range(tiles):
            j = i * tiles + t
            row = pl.multiple_of(at[j] * TILE, TILE)
            tile = jnp.where(
                here[j] != 0,
                late[pl.ds(row, TILE), :],
                mine[t * TILE : (t + 1) * TILE, span],
            )
            piece = tile.astype(F32) * prod[t * TILE : (t + 1) * TILE]
            part[:, span] += jnp.sum(piece, axis=0, keepdims=True)


def finish(acc, coeff, left, right, mine, source, wanted):
    rows, cols = acc.shape
    per = rows // TILE
    tiles = 2 if per % 2 == 0 else 1
    block = tiles * TILE
    rel = wanted - source * per
    here = ((rel >= 0) & (rel < per)).astype(jnp.int32)
    at = jnp.clip(rel, 0, per - 1)
    whole = lambda a: pl.BlockSpec(a.shape, lambda i, h, a: (0, 0))
    stripe = lambda a: pl.BlockSpec((block, a.shape[1]), lambda i, h, a: (i, 0))
    return pl.pallas_call(
        functools.partial(finish_kernel, tiles),
        grid_spec=pltpu.PrefetchScalarGridSpec(
            num_scalar_prefetch=2,
            grid=(per // tiles,),
            in_specs=[stripe(acc), stripe(coeff), whole(left), whole(right), stripe(mine)],
            out_specs=[stripe(acc), pl.BlockSpec((1, cols), lambda i, h, a: (0, 0))],
        ),
        out_shape=[
            jax.ShapeDtypeStruct((rows, cols), jnp.bfloat16),
            jax.ShapeDtypeStruct((1, cols), F32),
        ],
        compiler_params=pltpu.CompilerParams(vmem_limit_bytes=VMEM_LIMIT),
        cost_estimate=pl.CostEstimate(
            flops=2 * rows * cols * coeff.shape[1],
            bytes_accessed=8 * rows * cols + 4 * rows * coeff.shape[1],
            transcendentals=0,
        ),
    )(here, at, acc, coeff, left, right, mine)


def row_sum(value, n):
    step = 1
    if n & (n - 1):
        return lax.psum(value, "row")
    while step < n:
        value = value + lax.ppermute(value, "row", [(i, i ^ step) for i in range(n)])
        step *= 2
    return value


def body(sigma_anc, panel, holder, dinv_diag):
    n = lax.axis_size("row")
    me = lax.axis_index("row")
    rows, cols = panel.shape
    per = rows // TILE
    half = cols // 2
    order = list(range(0, n, 2)) + list(range(1, n, 2))[::-1]
    table = jnp.array(order, jnp.int32)
    place = jnp.array([order.index(i) for i in range(n)], jnp.int32)[me]
    fwd = [(order[i], order[(i + 1) % n]) for i in range(n)]
    bwd = [(b, a) for a, b in fwd]
    logical = jnp.argsort(holder).astype(jnp.int32)
    wanted = lax.dynamic_slice_in_dim(holder, me * per, per)

    whole = lax.all_gather(sigma_anc, "col", axis=1, tiled=True)
    sigma = reorder(whole, logical)

    def coeff(source):
        return lax.dynamic_slice_in_dim(sigma, source * rows, rows, axis=1)

    def term(source, piece):
        return jnp.dot(coeff(source), piece, preferred_element_type=F32)

    acc = term(me, panel)
    mine = pick([panel], [me], wanted, panel)
    a = b = panel
    for hop in range(1, n // 2):
        a, b = lax.ppermute(a, "row", fwd), lax.ppermute(b, "row", bwd)
        sources = [table[(place - hop) % n], table[(place + hop) % n]]
        acc = acc + term(sources[0], a)
        acc = acc + term(sources[1], b)
        mine = pick([a, b], sources, wanted, mine)
    left = lax.ppermute(a[:, :half], "row", fwd)
    right = lax.ppermute(b[:, half:], "row", bwd)
    source = table[(place + n // 2) % n]
    sigma_aj, part = finish(acc, coeff(source), left, right, mine, source, wanted)
    variances = dinv_diag + row_sum(part, n).reshape(cols)
    return sigma_aj, variances


def solution(mesh):
    placed = (
        P(("groups", "row"), "col"),
        P(("groups", "row"), "col"),
        P("groups"),
        P(("groups", "col")),
    )
    return jax.shard_map(
        body,
        mesh=mesh,
        in_specs=placed,
        out_specs=(P(("groups", "row"), "col"), P(("groups", "col"))),
        check_vma=False,
    )
```

```python
import functools

import jax
import jax.numpy as jnp
from jax import lax
from jax.experimental import pallas as pl
from jax.experimental.pallas import tpu as pltpu
from jax.sharding import PartitionSpec as P

TILE = 128
F32 = jnp.float32
VMEM_LIMIT = 56 * 1024 * 1024


def reorder_kernel(slots, a, o):
    o[...] = a[...]


def reorder(whole, logical):
    rows, width = whole.shape
    return pl.pallas_call(
        reorder_kernel,
        grid_spec=pltpu.PrefetchScalarGridSpec(
            num_scalar_prefetch=1,
            grid=(width // TILE,),
            in_specs=[pl.BlockSpec((rows, TILE), lambda k, t: (0, t[k]))],
            out_specs=pl.BlockSpec((rows, TILE), lambda k, t: (0, k)),
        ),
        out_shape=jax.ShapeDtypeStruct((rows, width), whole.dtype),
        cost_estimate=pl.CostEstimate(flops=0, bytes_accessed=4 * rows * width, transcendentals=0),
    )(logical, whole)


def pick_kernel(count, here, at, *refs):
    j = pl.program_id(0)
    pieces, base, out = refs[:count], refs[count], refs[count + 1]
    value = base[...]
    for p in range(count):
        value = jnp.where(here[p, j] != 0, pieces[p][...], value)
    out[...] = value


def pick(pieces, sources, wanted, base):
    rows, cols = base.shape
    per = rows // TILE
    rel = jnp.stack([wanted - s * per for s in sources])
    here = ((rel >= 0) & (rel < per)).astype(jnp.int32)
    at = jnp.clip(rel, 0, per - 1)
    count = len(pieces)
    specs = [
        pl.BlockSpec((TILE, cols), functools.partial(lambda p, j, h, a: (a[p, j], 0), p))
        for p in range(count)
    ]
    tile = pl.BlockSpec((TILE, cols), lambda j, h, a: (j, 0))
    return pl.pallas_call(
        functools.partial(pick_kernel, count),
        grid_spec=pltpu.PrefetchScalarGridSpec(
            num_scalar_prefetch=2,
            grid=(per,),
            in_specs=specs + [tile],
            out_specs=tile,
        ),
        out_shape=jax.ShapeDtypeStruct((rows, cols), base.dtype),
        cost_estimate=pl.CostEstimate(
            flops=0, bytes_accessed=2 * (count + 2) * rows * cols, transcendentals=0
        ),
    )(here, at, *pieces, base)


def finish_kernel(tiles, here, at, acc, coeff, left, right, mine, out, part):
    i = pl.program_id(0)

    @pl.when(i == 0)
    def _():
        part[...] = jnp.zeros_like(part)

    half = left.shape[1]
    for late, lo in ((left, 0), (right, half)):
        span = pl.ds(lo, half)
        prod = acc[:, span] + jnp.dot(coeff[...], late[...], preferred_element_type=F32)
        out[:, span] = (-prod).astype(out.dtype)
        for t in range(tiles):
            j = i * tiles + t
            row = pl.multiple_of(at[j] * TILE, TILE)
            tile = jnp.where(
                here[j] != 0,
                late[pl.ds(row, TILE), :],
                mine[t * TILE : (t + 1) * TILE, span],
            )
            piece = tile.astype(F32) * prod[t * TILE : (t + 1) * TILE]
            part[:, span] += jnp.sum(piece, axis=0, keepdims=True)


def finish(acc, coeff, left, right, mine, source, wanted):
    rows, cols = acc.shape
    per = rows // TILE
    tiles = 2 if per % 2 == 0 else 1
    block = tiles * TILE
    rel = wanted - source * per
    here = ((rel >= 0) & (rel < per)).astype(jnp.int32)
    at = jnp.clip(rel, 0, per - 1)
    whole = lambda a: pl.BlockSpec(a.shape, lambda i, h, a: (0, 0))
    stripe = lambda a: pl.BlockSpec((block, a.shape[1]), lambda i, h, a: (i, 0))
    return pl.pallas_call(
        functools.partial(finish_kernel, tiles),
        grid_spec=pltpu.PrefetchScalarGridSpec(
            num_scalar_prefetch=2,
            grid=(per // tiles,),
            in_specs=[stripe(acc), stripe(coeff), whole(left), whole(right), stripe(mine)],
            out_specs=[stripe(acc), pl.BlockSpec((1, cols), lambda i, h, a: (0, 0))],
        ),
        out_shape=[
            jax.ShapeDtypeStruct((rows, cols), jnp.bfloat16),
            jax.ShapeDtypeStruct((1, cols), F32),
        ],
        compiler_params=pltpu.CompilerParams(vmem_limit_bytes=VMEM_LIMIT),
        cost_estimate=pl.CostEstimate(
            flops=2 * rows * cols * coeff.shape[1],
            bytes_accessed=8 * rows * cols + 4 * rows * coeff.shape[1],
            transcendentals=0,
        ),
    )(here, at, acc, coeff, left, right, mine)


def row_sum(value, n):
    step = 1
    if n & (n - 1):
        return lax.psum(value, "row")
    while step < n:
        value = value + lax.ppermute(value, "row", [(i, i ^ step) for i in range(n)])
        step *= 2
    return value


def body(sigma_anc, panel, holder, dinv_diag):
    n = lax.axis_size("row")
    me = lax.axis_index("row")
    rows, cols = panel.shape
    per = rows // TILE
    half = cols // 2
    order = list(range(0, n, 2)) + list(range(1, n, 2))[::-1]
    table = jnp.array(order, jnp.int32)
    place = jnp.array([order.index(i) for i in range(n)], jnp.int32)[me]
    fwd = [(order[i], order[(i + 1) % n]) for i in range(n)]
    bwd = [(b, a) for a, b in fwd]
    logical = jnp.argsort(holder).astype(jnp.int32)
    wanted = lax.dynamic_slice_in_dim(holder, me * per, per)

    whole = lax.all_gather(sigma_anc, "col", axis=1, tiled=True)
    sigma = reorder(whole, logical)

    def coeff(source):
        return lax.dynamic_slice_in_dim(sigma, source * rows, rows, axis=1)

    def term(source, piece):
        return jnp.dot(coeff(source), piece, preferred_element_type=F32)

    mine = pick([panel], [me], wanted, panel)
    a = b = panel
    acc = None
    ready, fresh = [(me, panel)], []
    for hop in range(1, n // 2 + 1):
        if hop == 2:
            a, b, mine, sigma = lax.optimization_barrier((a, b, mine, sigma))
        if hop > 2:
            for source, piece in ready:
                update = term(source, piece)
                acc = update if acc is None else acc + update
            mine = pick([p for _, p in ready], [s for s, _ in ready], wanted, mine)
            a, b, acc, mine = lax.optimization_barrier((a, b, acc, mine))
            ready = []
        ready, fresh = ready + fresh, []
        if hop == n // 2:
            break
        a, b = lax.ppermute(a, "row", fwd), lax.ppermute(b, "row", bwd)
        fresh = [(table[(place - hop) % n], a), (table[(place + hop) % n], b)]
    left = lax.ppermute(a[:, :half], "row", fwd)
    right = lax.ppermute(b[:, half:], "row", bwd)
    for source, piece in ready:
        update = term(source, piece)
        acc = update if acc is None else acc + update
    mine = pick([p for _, p in ready], [s for s, _ in ready], wanted, mine)
    left, right, acc, mine = lax.optimization_barrier((left, right, acc, mine))
    source = table[(place + n // 2) % n]
    sigma_aj, part = finish(acc, coeff(source), left, right, mine, source, wanted)
    variances = dinv_diag + row_sum(part, n).reshape(cols)
    return sigma_aj, variances


def solution(mesh):
    placed = (
        P(("groups", "row"), "col"),
        P(("groups", "row"), "col"),
        P("groups"),
        P(("groups", "col")),
    )
    return jax.shard_map(
        body,
        mesh=mesh,
        in_specs=placed,
        out_specs=(P(("groups", "row"), "col"), P(("groups", "col"))),
        check_vma=False,
    )
```

```python
import functools

import jax
import jax.numpy as jnp
from jax import lax
from jax.experimental import pallas as pl
from jax.experimental.pallas import tpu as pltpu
from jax.sharding import PartitionSpec as P

TILE = 128
F32 = jnp.float32
VMEM_LIMIT = 56 * 1024 * 1024


def reorder_kernel(side, at, own, other, out):
    k = pl.program_id(0)
    out[...] = jnp.where(side[k] == 0, own[...], other[...])


def reorder(own, other, logical):
    rows, half = own.shape
    per_half = half // TILE
    side = (logical // per_half != lax.axis_index("col")).astype(jnp.int32)
    step = jnp.arange(2 * per_half, dtype=jnp.int32)
    upto = step[None, :] <= step[:, None]
    last = lambda flag: jnp.max(jnp.where(upto & flag[None, :], step[None, :], 0), axis=1)
    at = (logical % per_half)[jnp.stack([last(side == 0), last(side == 1)])]
    tile = lambda p: pl.BlockSpec((rows, TILE), functools.partial(lambda p, k, s, a: (0, a[p, k]), p))
    return pl.pallas_call(
        reorder_kernel,
        grid_spec=pltpu.PrefetchScalarGridSpec(
            num_scalar_prefetch=2,
            grid=(2 * per_half,),
            in_specs=[tile(0), tile(1)],
            out_specs=pl.BlockSpec((rows, TILE), lambda k, s, a: (0, k)),
        ),
        out_shape=jax.ShapeDtypeStruct((rows, 2 * half), own.dtype),
        cost_estimate=pl.CostEstimate(flops=0, bytes_accessed=rows * half, transcendentals=0),
    )(side, at, own, other)


def found(wanted, source, per):
    rel = wanted - source * per
    here = ((rel >= 0) & (rel < per)).astype(jnp.int32)
    return here, jnp.clip(rel, 0, per - 1)


def tile_rows(at):
    return pl.ds(pl.multiple_of(at * TILE, TILE), TILE)


def accumulate_kernel(count, first, blocks, source, here, at, *refs):
    sigmas, pieces = refs[:count], refs[count : 3 * count]
    acc_in, mine_in = (None, None) if first else refs[3 * count : 3 * count + 2]
    acc, mine = refs[-2:]
    j = pl.program_id(0)
    for side in range(2):

        @pl.when(j // blocks == side)
        def _():
            for p in range(count):
                term = jnp.dot(sigmas[p][...], pieces[2 * p + side][...], preferred_element_type=F32)
                if p > 0:
                    acc[...] += term
                elif first:
                    acc[...] = term
                else:
                    acc[...] = acc_in[...] + term
            for t in range(acc.shape[0] // TILE):
                rows = slice(t * TILE, (t + 1) * TILE)
                value = None if first else mine_in[rows, :]
                for p in range(count):
                    got = pieces[2 * p + side][tile_rows(at[p, t]), :]
                    value = got if value is None else jnp.where(here[p, t] != 0, got, value)
                mine[rows, :] = value


def sides(rows, unit, blocks):
    left = pl.BlockSpec((rows, unit), lambda j, *_: (0, jnp.minimum(j, blocks - 1)))
    right = pl.BlockSpec((rows, unit), lambda j, *_: (0, jnp.maximum(j - blocks, 0)))
    return [left, right]


def accumulate(sigma, sources, pieces, wanted, state, unit):
    count = len(sources)
    first = state is None
    rows, half = pieces[0][0].shape
    blocks = half // unit
    per = rows // TILE
    marks = [found(wanted, s, per) for s in sources]
    here = jnp.stack([m[0] for m in marks])
    at = jnp.stack([m[1] for m in marks])
    cut = pl.BlockSpec((rows, unit), lambda j, *_: (0, j))
    sigma_specs = [
        pl.BlockSpec((rows, rows), functools.partial(lambda p, j, s, *_: (0, s[p]), p))
        for p in range(count)
    ]
    flat = [x for pair in pieces for x in pair]
    extra = [] if first else list(state)
    start = 3 + 3 * count
    return pl.pallas_call(
        functools.partial(accumulate_kernel, count, first, blocks),
        grid_spec=pltpu.PrefetchScalarGridSpec(
            num_scalar_prefetch=3,
            grid=(2 * blocks,),
            in_specs=sigma_specs + sides(rows, unit, blocks) * count + [cut] * len(extra),
            out_specs=[cut, cut],
        ),
        out_shape=[
            jax.ShapeDtypeStruct((rows, 2 * half), F32),
            jax.ShapeDtypeStruct((rows, 2 * half), flat[0].dtype),
        ],
        input_output_aliases={} if first else {start: 0, start + 1: 1},
        compiler_params=pltpu.CompilerParams(vmem_limit_bytes=VMEM_LIMIT),
        cost_estimate=pl.CostEstimate(flops=count * rows * half, bytes_accessed=rows * half, transcendentals=0),
    )(jnp.stack(sources), here, at, *([sigma] * count), *flat, *extra)


def finish_kernel(blocks, source, here, at, sigma, left, right, acc, mine, out, part):
    j = pl.program_id(0)
    for side, late in enumerate((left, right)):

        @pl.when(j // blocks == side)
        def _():
            prod = acc[...] + jnp.dot(sigma[...], late[...], preferred_element_type=F32)
            out[...] = (-prod).astype(out.dtype)
            total = None
            for t in range(acc.shape[0] // TILE):
                rows = slice(t * TILE, (t + 1) * TILE)
                tile = jnp.where(here[t] != 0, late[tile_rows(at[t]), :], mine[rows, :])
                add = tile.astype(F32) * prod[rows]
                total = add if total is None else total + add
            part[...] = jnp.sum(total, axis=0, keepdims=True)


def finish(sigma, source, left, right, state, wanted, unit):
    acc, mine = state
    rows, cols = acc.shape
    blocks = left.shape[1] // unit
    here, at = found(wanted, source, rows // TILE)
    cut = pl.BlockSpec((rows, unit), lambda j, *_: (0, j))
    return pl.pallas_call(
        functools.partial(finish_kernel, blocks),
        grid_spec=pltpu.PrefetchScalarGridSpec(
            num_scalar_prefetch=3,
            grid=(2 * blocks,),
            in_specs=[pl.BlockSpec((rows, rows), lambda j, s, *_: (0, s[0]))]
            + sides(rows, unit, blocks)
            + [cut, cut],
            out_specs=[cut, pl.BlockSpec((1, unit), lambda j, *_: (0, j))],
        ),
        out_shape=[
            jax.ShapeDtypeStruct((rows, cols), jnp.bfloat16),
            jax.ShapeDtypeStruct((1, cols), F32),
        ],
        compiler_params=pltpu.CompilerParams(vmem_limit_bytes=VMEM_LIMIT),
        cost_estimate=pl.CostEstimate(flops=rows * cols, bytes_accessed=rows * cols, transcendentals=0),
    )(source[None], here, at, sigma, left, right, acc, mine)


def row_sum(value, n):
    step = 1
    if n & (n - 1):
        return lax.psum(value, "row")
    while step < n:
        value = value + lax.ppermute(value, "row", [(i, i ^ step) for i in range(n)])
        step *= 2
    return value


def body(sigma_anc, panel, holder, dinv_diag):
    n = lax.axis_size("row")
    me = lax.axis_index("row")
    rows, cols = panel.shape
    per = rows // TILE
    half = cols // 2
    unit = half // 3 if half % (3 * TILE) == 0 else half
    order = list(range(0, n, 2)) + list(range(1, n, 2))[::-1]
    table = jnp.array(order, jnp.int32)
    place = jnp.array([order.index(i) for i in range(n)], jnp.int32)[me]
    fwd = [(order[i], order[(i + 1) % n]) for i in range(n)]
    bwd = [(b, a) for a, b in fwd]
    ahead = lambda x: lax.ppermute(x, "row", fwd)
    back = lambda x: lax.ppermute(x, "row", bwd)
    wanted = lax.dynamic_slice_in_dim(holder, me * per, per)
    tile_ids = jnp.arange(holder.shape[0], dtype=jnp.int32)
    logical = jnp.sum(
        jnp.where(holder[:, None] == tile_ids[None, :], tile_ids[:, None], 0), axis=0
    )

    own = (panel[:, :half], panel[:, half:])
    (al, ar), (bl, br) = own, own
    state = None
    ready = [(me, own)]
    sigma = None
    for hop in range(1, n // 2):
        if hop > 2:
            state = accumulate(sigma, [s for s, _ in ready], [p for _, p in ready], wanted, state, unit)
            ready = []
            al, br, state = lax.optimization_barrier((al, br, state))
        al, br = ahead(al), back(br)
        if hop == 1:
            other = lax.ppermute(sigma_anc, "col", [(0, 1), (1, 0)])
            sigma = reorder(sigma_anc, other, logical)
        if hop == 2:
            ar, bl, sigma = lax.optimization_barrier((ar, bl, sigma))
        ar, bl = ahead(ar), back(bl)
        sources = [table[(place - hop) % n], table[(place + hop) % n]]
        if hop > 1:
            ready += fresh
        fresh = [(sources[0], (al, ar)), (sources[1], (bl, br))]
    state = accumulate(sigma, [s for s, _ in ready], [p for _, p in ready], wanted, state, unit)
    al, br, state = lax.optimization_barrier((al, br, state))
    al, br = ahead(al), back(br)
    state = accumulate(sigma, [s for s, _ in fresh], [p for _, p in fresh], wanted, state, unit)
    al, br, state = lax.optimization_barrier((al, br, state))
    source = table[(place + n // 2) % n]
    out, part = finish(sigma, source, al, br, state, wanted, unit)
    return out, dinv_diag + row_sum(part, n).reshape(cols)


def solution(mesh):
    placed = (
        P(("groups", "row"), "col"),
        P(("groups", "row"), "col"),
        P("groups"),
        P(("groups", "col")),
    )
    return jax.shard_map(
        body,
        mesh=mesh,
        in_specs=placed,
        out_specs=(P(("groups", "row"), "col"), P(("groups", "col"))),
        check_vma=False,
    )
```

```python
import functools

import jax
import jax.numpy as jnp
from jax import lax
from jax.experimental import pallas as pl
from jax.experimental.pallas import tpu as pltpu
from jax.sharding import PartitionSpec as P

TILE = 128
F32 = jnp.float32
VMEM_LIMIT = 28 * 1024 * 1024


def reorder_kernel(side, at, own, other, out):
    k = pl.program_id(0)
    out[...] = jnp.where(side[k] == 0, own[...], other[...])


def reorder(own, other, logical):
    rows, half = own.shape
    per_half = half // TILE
    side = (logical // per_half != lax.axis_index("col")).astype(jnp.int32)
    step = jnp.arange(2 * per_half, dtype=jnp.int32)
    upto = step[None, :] <= step[:, None]
    last = lambda flag: jnp.max(jnp.where(upto & flag[None, :], step[None, :], 0), axis=1)
    at = (logical % per_half)[jnp.stack([last(side == 0), last(side == 1)])]
    tile = lambda p: pl.BlockSpec((rows, TILE), functools.partial(lambda p, k, s, a: (0, a[p, k]), p))
    return pl.pallas_call(
        reorder_kernel,
        grid_spec=pltpu.PrefetchScalarGridSpec(
            num_scalar_prefetch=2,
            grid=(2 * per_half,),
            in_specs=[tile(0), tile(1)],
            out_specs=pl.BlockSpec((rows, TILE), lambda k, s, a: (0, k)),
        ),
        out_shape=jax.ShapeDtypeStruct((rows, 2 * half), own.dtype),
        cost_estimate=pl.CostEstimate(flops=0, bytes_accessed=rows * half, transcendentals=0),
    )(side, at, own, other)


def found(wanted, source, per):
    rel = wanted - source * per
    here = ((rel >= 0) & (rel < per)).astype(jnp.int32)
    return here, jnp.clip(rel, 0, per - 1)


def tile_rows(at):
    return pl.ds(pl.multiple_of(at * TILE, TILE), TILE)


def accumulate_kernel(count, first, blocks, source, here, at, *refs):
    sigmas, pieces = refs[:count], refs[count : 3 * count]
    acc_in, mine_in = (None, None) if first else refs[3 * count : 3 * count + 2]
    acc, mine = refs[-2:]
    j = pl.program_id(0)
    for side in range(2):

        @pl.when(j // blocks == side)
        def _():
            for p in range(count):
                term = jnp.dot(sigmas[p][...], pieces[2 * p + side][...], preferred_element_type=F32)
                if p > 0:
                    acc[...] += term
                elif first:
                    acc[...] = term
                else:
                    acc[...] = acc_in[...] + term
            for t in range(acc.shape[0] // TILE):
                rows = slice(t * TILE, (t + 1) * TILE)
                value = None if first else mine_in[rows, :]
                for p in range(count):
                    got = pieces[2 * p + side][tile_rows(at[p, t]), :]
                    value = got if value is None else jnp.where(here[p, t] != 0, got, value)
                mine[rows, :] = value


def sides(rows, unit, blocks):
    left = pl.BlockSpec((rows, unit), lambda j, *_: (0, jnp.minimum(j, blocks - 1)))
    right = pl.BlockSpec((rows, unit), lambda j, *_: (0, jnp.maximum(j - blocks, 0)))
    return [left, right]


def accumulate(sigma, sources, pieces, wanted, state, unit):
    count = len(sources)
    first = state is None
    rows, half = pieces[0][0].shape
    blocks = half // unit
    per = rows // TILE
    marks = [found(wanted, s, per) for s in sources]
    here = jnp.stack([m[0] for m in marks])
    at = jnp.stack([m[1] for m in marks])
    cut = pl.BlockSpec((rows, unit), lambda j, *_: (0, j))
    sigma_specs = [
        pl.BlockSpec((rows, rows), functools.partial(lambda p, j, s, *_: (0, s[p]), p))
        for p in range(count)
    ]
    flat = [x for pair in pieces for x in pair]
    extra = [] if first else list(state)
    start = 3 + 3 * count
    return pl.pallas_call(
        functools.partial(accumulate_kernel, count, first, blocks),
        grid_spec=pltpu.PrefetchScalarGridSpec(
            num_scalar_prefetch=3,
            grid=(2 * blocks,),
            in_specs=sigma_specs + sides(rows, unit, blocks) * count + [cut] * len(extra),
            out_specs=[cut, cut],
        ),
        out_shape=[
            jax.ShapeDtypeStruct((rows, 2 * half), F32),
            jax.ShapeDtypeStruct((rows, 2 * half), flat[0].dtype),
        ],
        input_output_aliases={} if first else {start: 0, start + 1: 1},
        compiler_params=pltpu.CompilerParams(vmem_limit_bytes=VMEM_LIMIT),
        cost_estimate=pl.CostEstimate(flops=count * rows * half, bytes_accessed=rows * half, transcendentals=0),
    )(jnp.stack(sources), here, at, *([sigma] * count), *flat, *extra)


def finish_kernel(blocks, source, here, at, sigma, left, right, acc, mine, out, part):
    j = pl.program_id(0)
    for side, late in enumerate((left, right)):

        @pl.when(j // blocks == side)
        def _():
            prod = acc[...] + jnp.dot(sigma[...], late[...], preferred_element_type=F32)
            out[...] = (-prod).astype(out.dtype)
            total = None
            for t in range(acc.shape[0] // TILE):
                rows = slice(t * TILE, (t + 1) * TILE)
                tile = jnp.where(here[t] != 0, late[tile_rows(at[t]), :], mine[rows, :])
                add = tile.astype(F32) * prod[rows]
                total = add if total is None else total + add
            part[...] = jnp.sum(total, axis=0, keepdims=True)


def finish(sigma, source, left, right, state, wanted, unit):
    acc, mine = state
    rows, cols = acc.shape
    blocks = left.shape[1] // unit
    here, at = found(wanted, source, rows // TILE)
    cut = pl.BlockSpec((rows, unit), lambda j, *_: (0, j))
    return pl.pallas_call(
        functools.partial(finish_kernel, blocks),
        grid_spec=pltpu.PrefetchScalarGridSpec(
            num_scalar_prefetch=3,
            grid=(2 * blocks,),
            in_specs=[pl.BlockSpec((rows, rows), lambda j, s, *_: (0, s[0]))]
            + sides(rows, unit, blocks)
            + [cut, cut],
            out_specs=[cut, pl.BlockSpec((1, unit), lambda j, *_: (0, j))],
        ),
        out_shape=[
            jax.ShapeDtypeStruct((rows, cols), jnp.bfloat16),
            jax.ShapeDtypeStruct((1, cols), F32),
        ],
        compiler_params=pltpu.CompilerParams(vmem_limit_bytes=VMEM_LIMIT),
        cost_estimate=pl.CostEstimate(flops=rows * cols, bytes_accessed=rows * cols, transcendentals=0),
    )(source[None], here, at, sigma, left, right, acc, mine)


def row_sum(value, n):
    step = 1
    if n & (n - 1):
        return lax.psum(value, "row")
    while step < n:
        value = value + lax.ppermute(value, "row", [(i, i ^ step) for i in range(n)])
        step *= 2
    return value


def body(sigma_anc, panel, holder, dinv_diag):
    n = lax.axis_size("row")
    me = lax.axis_index("row")
    rows, cols = panel.shape
    per = rows // TILE
    half = cols // 2
    unit = half // 3 if half % (3 * TILE) == 0 else half
    order = list(range(0, n, 2)) + list(range(1, n, 2))[::-1]
    table = jnp.array(order, jnp.int32)
    place = jnp.array([order.index(i) for i in range(n)], jnp.int32)[me]
    fwd = [(order[i], order[(i + 1) % n]) for i in range(n)]
    bwd = [(b, a) for a, b in fwd]
    ahead = lambda x: lax.ppermute(x, "row", fwd)
    back = lambda x: lax.ppermute(x, "row", bwd)
    wanted = lax.dynamic_slice_in_dim(holder, me * per, per)
    tile_ids = jnp.arange(holder.shape[0], dtype=jnp.int32)
    logical = jnp.sum(
        jnp.where(holder[:, None] == tile_ids[None, :], tile_ids[:, None], 0), axis=0
    )

    own = (panel[:, :half], panel[:, half:])
    (al, ar), (bl, br) = own, own
    state = None
    ready = [(me, own)]
    sigma = None
    for hop in range(1, n // 2):
        if hop > 2:
            state = accumulate(sigma, [s for s, _ in ready], [p for _, p in ready], wanted, state, unit)
            ready = []
            al, br, state = lax.optimization_barrier((al, br, state))
        al, br = ahead(al), back(br)
        if hop == 1:
            other = lax.ppermute(sigma_anc, "col", [(0, 1), (1, 0)])
            sigma = reorder(sigma_anc, other, logical)
        if hop == 2:
            ar, bl, sigma = lax.optimization_barrier((ar, bl, sigma))
        ar, bl = ahead(ar), back(bl)
        sources = [table[(place - hop) % n], table[(place + hop) % n]]
        if hop > 1:
            ready += fresh
        fresh = [(sources[0], (al, ar)), (sources[1], (bl, br))]
    state = accumulate(sigma, [s for s, _ in ready], [p for _, p in ready], wanted, state, unit)
    al, br, state = lax.optimization_barrier((al, br, state))
    al, br = ahead(al), back(br)
    state = accumulate(sigma, [s for s, _ in fresh], [p for _, p in fresh], wanted, state, unit)
    al, br, state = lax.optimization_barrier((al, br, state))
    source = table[(place + n // 2) % n]
    out, part = finish(sigma, source, al, br, state, wanted, unit)
    return out, dinv_diag + row_sum(part, n).reshape(cols)


def solution(mesh):
    placed = (
        P(("groups", "row"), "col"),
        P(("groups", "row"), "col"),
        P("groups"),
        P(("groups", "col")),
    )
    return jax.shard_map(
        body,
        mesh=mesh,
        in_specs=placed,
        out_specs=(P(("groups", "row"), "col"), P(("groups", "col"))),
        check_vma=False,
    )
```

```python
import functools

import jax
import jax.numpy as jnp
from jax import lax
from jax.experimental import pallas as pl
from jax.experimental.pallas import tpu as pltpu
from jax.sharding import PartitionSpec as P

TILE = 128
F32 = jnp.float32
VMEM_LIMIT = 28 * 1024 * 1024


def reorder_kernel(side, at, own, other, out):
    k = pl.program_id(0)
    out[...] = jnp.where(side[k] == 0, own[...], other[...])


def reorder(own, other, logical):
    rows, half = own.shape
    per_half = half // TILE
    side = (logical // per_half != lax.axis_index("col")).astype(jnp.int32)
    step = jnp.arange(2 * per_half, dtype=jnp.int32)
    upto = step[None, :] <= step[:, None]
    last = lambda flag: jnp.max(jnp.where(upto & flag[None, :], step[None, :], 0), axis=1)
    at = (logical % per_half)[jnp.stack([last(side == 0), last(side == 1)])]
    tile = lambda p: pl.BlockSpec((rows, TILE), functools.partial(lambda p, k, s, a: (0, a[p, k]), p))
    return pl.pallas_call(
        reorder_kernel,
        grid_spec=pltpu.PrefetchScalarGridSpec(
            num_scalar_prefetch=2,
            grid=(2 * per_half,),
            in_specs=[tile(0), tile(1)],
            out_specs=pl.BlockSpec((rows, TILE), lambda k, s, a: (0, k)),
        ),
        out_shape=jax.ShapeDtypeStruct((rows, 2 * half), own.dtype),
        cost_estimate=pl.CostEstimate(flops=0, bytes_accessed=rows * half, transcendentals=0),
    )(side, at, own, other)


def found(wanted, source, per):
    rel = wanted - source * per
    here = ((rel >= 0) & (rel < per)).astype(jnp.int32)
    return here, jnp.clip(rel, 0, per - 1)


def tile_rows(at):
    return pl.ds(pl.multiple_of(at * TILE, TILE), TILE)


def accumulate_kernel(count, first, blocks, source, here, at, *refs):
    sigmas, pieces = refs[:count], refs[count : 3 * count]
    acc_in, mine_in = (None, None) if first else refs[3 * count : 3 * count + 2]
    acc, mine = refs[-2:]
    j = pl.program_id(0)
    for side in range(2):

        @pl.when(j // blocks == side)
        def _():
            for p in range(count):
                term = jnp.dot(sigmas[p][...], pieces[2 * p + side][...], preferred_element_type=F32)
                if p > 0:
                    acc[...] += term
                elif first:
                    acc[...] = term
                else:
                    acc[...] = acc_in[...] + term
            for t in range(acc.shape[0] // TILE):
                rows = slice(t * TILE, (t + 1) * TILE)
                value = None if first else mine_in[rows, :]
                for p in range(count):
                    got = pieces[2 * p + side][tile_rows(at[p, t]), :]
                    value = got if value is None else jnp.where(here[p, t] != 0, got, value)
                mine[rows, :] = value


def sides(rows, unit, blocks):
    left = pl.BlockSpec((rows, unit), lambda j, *_: (0, jnp.minimum(j, blocks - 1)))
    right = pl.BlockSpec((rows, unit), lambda j, *_: (0, jnp.maximum(j - blocks, 0)))
    return [left, right]


def accumulate(sigma, sources, pieces, wanted, state, unit):
    count = len(sources)
    first = state is None
    rows, half = pieces[0][0].shape
    blocks = half // unit
    per = rows // TILE
    marks = [found(wanted, s, per) for s in sources]
    here = jnp.stack([m[0] for m in marks])
    at = jnp.stack([m[1] for m in marks])
    cut = pl.BlockSpec((rows, unit), lambda j, *_: (0, j))
    sigma_specs = [
        pl.BlockSpec((rows, rows), functools.partial(lambda p, j, s, *_: (0, s[p]), p))
        for p in range(count)
    ]
    flat = [x for pair in pieces for x in pair]
    extra = [] if first else list(state)
    start = 3 + 3 * count
    return pl.pallas_call(
        functools.partial(accumulate_kernel, count, first, blocks),
        grid_spec=pltpu.PrefetchScalarGridSpec(
            num_scalar_prefetch=3,
            grid=(2 * blocks,),
            in_specs=sigma_specs + sides(rows, unit, blocks) * count + [cut] * len(extra),
            out_specs=[cut, cut],
        ),
        out_shape=[
            jax.ShapeDtypeStruct((rows, 2 * half), F32),
            jax.ShapeDtypeStruct((rows, 2 * half), flat[0].dtype),
        ],
        input_output_aliases={} if first else {start: 0, start + 1: 1},
        compiler_params=pltpu.CompilerParams(vmem_limit_bytes=VMEM_LIMIT),
        cost_estimate=pl.CostEstimate(flops=count * rows * half, bytes_accessed=rows * half, transcendentals=0),
    )(jnp.stack(sources), here, at, *([sigma] * count), *flat, *extra)


def finish_kernel(blocks, here, at, sigma, left, right, acc, mine, *refs):
    out, part = refs[-2:]
    j = pl.program_id(0)
    for side, late in enumerate((left, right)):

        @pl.when(j // blocks == side)
        def _():
            prod = acc[...] + jnp.dot(sigma[...], late[...], preferred_element_type=F32)
            out[...] = (-prod).astype(out.dtype)
            total = None
            for t in range(acc.shape[0] // TILE):
                rows = slice(t * TILE, (t + 1) * TILE)
                tile = jnp.where(here[t] != 0, late[tile_rows(at[t]), :], mine[rows, :])
                add = tile.astype(F32) * prod[rows]
                total = add if total is None else total + add
            part[...] = jnp.sum(total, axis=0, keepdims=True)


def finish(coeff, source, left, right, state, wanted, unit, begin, out):
    acc, mine = state
    rows, cols = acc.shape
    width = left.shape[1]
    blocks = width // unit
    here, at = found(wanted, source, rows // TILE)
    first, second = begin // unit, (cols // 2 + begin) // unit - blocks
    cut = pl.BlockSpec((rows, unit), lambda j, *_: (0, j + jnp.where(j < blocks, first, second)))
    extra = [] if out is None else [out]
    return pl.pallas_call(
        functools.partial(finish_kernel, blocks),
        grid_spec=pltpu.PrefetchScalarGridSpec(
            num_scalar_prefetch=2,
            grid=(2 * blocks,),
            in_specs=[pl.BlockSpec((rows, rows), lambda j, *_: (0, 0))]
            + sides(rows, unit, blocks)
            + [cut, cut]
            + [pl.BlockSpec(memory_space=pl.ANY)] * len(extra),
            out_specs=[cut, pl.BlockSpec((1, unit), lambda j, *_: (0, j))],
        ),
        out_shape=[
            jax.ShapeDtypeStruct((rows, cols), jnp.bfloat16),
            jax.ShapeDtypeStruct((1, 2 * width), F32),
        ],
        input_output_aliases={} if out is None else {7: 0},
        compiler_params=pltpu.CompilerParams(vmem_limit_bytes=VMEM_LIMIT),
        cost_estimate=pl.CostEstimate(flops=rows * width, bytes_accessed=rows * width, transcendentals=0),
    )(here, at, coeff, left, right, acc, mine, *extra)


def row_sum(value, n):
    step = 1
    if n & (n - 1):
        return lax.psum(value, "row")
    while step < n:
        value = value + lax.ppermute(value, "row", [(i, i ^ step) for i in range(n)])
        step *= 2
    return value


def body(sigma_anc, panel, holder, dinv_diag):
    n = lax.axis_size("row")
    me = lax.axis_index("row")
    rows, cols = panel.shape
    per = rows // TILE
    half = cols // 2
    unit = half // 3 if half % (3 * TILE) == 0 else half
    order = list(range(0, n, 2)) + list(range(1, n, 2))[::-1]
    table = jnp.array(order, jnp.int32)
    place = jnp.array([order.index(i) for i in range(n)], jnp.int32)[me]
    fwd = [(order[i], order[(i + 1) % n]) for i in range(n)]
    bwd = [(b, a) for a, b in fwd]
    ahead = lambda x: lax.ppermute(x, "row", fwd)
    back = lambda x: lax.ppermute(x, "row", bwd)
    wanted = lax.dynamic_slice_in_dim(holder, me * per, per)
    tile_ids = jnp.arange(holder.shape[0], dtype=jnp.int32)
    logical = jnp.sum(
        jnp.where(holder[:, None] == tile_ids[None, :], tile_ids[:, None], 0), axis=0
    )

    own = (panel[:, :half], panel[:, half:])
    (al, ar), (bl, br) = own, own
    state = None
    ready = [(me, own)]
    sigma = None
    for hop in range(1, n // 2):
        if hop > 2:
            state = accumulate(sigma, [s for s, _ in ready], [p for _, p in ready], wanted, state, unit)
            ready = []
            al, br, state = lax.optimization_barrier((al, br, state))
        al, br = ahead(al), back(br)
        if hop == 1:
            other = lax.ppermute(sigma_anc, "col", [(0, 1), (1, 0)])
            sigma = reorder(sigma_anc, other, logical)
        if hop == 2:
            ar, bl, sigma = lax.optimization_barrier((ar, bl, sigma))
        ar, bl = ahead(ar), back(bl)
        sources = [table[(place - hop) % n], table[(place + hop) % n]]
        if hop > 1:
            ready += fresh
        fresh = [(sources[0], (al, ar)), (sources[1], (bl, br))]
    state = accumulate(sigma, [s for s, _ in ready], [p for _, p in ready], wanted, state, unit)
    al, br, state = lax.optimization_barrier((al, br, state))
    splits = [(0, half - unit), (half - unit, unit)] if unit < half else [(0, half)]
    late = [(ahead(al[:, lo : lo + w]), back(br[:, lo : lo + w])) for lo, w in splits]
    state = accumulate(sigma, [s for s, _ in fresh], [p for _, p in fresh], wanted, state, unit)
    source = table[(place + n // 2) % n]
    coeff = lax.dynamic_slice_in_dim(sigma, source * rows, rows, axis=1)
    out, parts = None, []
    for (lo, w), (left, right) in zip(splits, late):

        out, part = finish(coeff, source, left, right, state, wanted, unit, lo, out)
        parts.append((part[:, :w], part[:, w:]))
    part = jnp.concatenate([p for p, _ in parts] + [p for _, p in parts], axis=1)
    return out, dinv_diag + row_sum(part, n).reshape(cols)


def solution(mesh):
    placed = (
        P(("groups", "row"), "col"),
        P(("groups", "row"), "col"),
        P("groups"),
        P(("groups", "col")),
    )
    return jax.shard_map(
        body,
        mesh=mesh,
        in_specs=placed,
        out_specs=(P(("groups", "row"), "col"), P(("groups", "col"))),
        check_vma=False,
    )
```

```python
import functools

import jax
import jax.numpy as jnp
from jax import lax
from jax.experimental import pallas as pl
from jax.experimental.pallas import tpu as pltpu
from jax.sharding import PartitionSpec as P

TILE = 128
F32 = jnp.float32
VMEM_LIMIT = 28 * 1024 * 1024


def reorder_kernel(side, at, own, other, out):
    k = pl.program_id(0)
    out[...] = jnp.where(side[k] == 0, own[...], other[...])


def reorder(own, other, logical):
    rows, half = own.shape
    per_half = half // TILE
    side = (logical // per_half != lax.axis_index("col")).astype(jnp.int32)
    step = jnp.arange(2 * per_half, dtype=jnp.int32)
    upto = step[None, :] <= step[:, None]
    last = lambda flag: jnp.max(jnp.where(upto & flag[None, :], step[None, :], 0), axis=1)
    at = (logical % per_half)[jnp.stack([last(side == 0), last(side == 1)])]
    tile = lambda p: pl.BlockSpec((rows, TILE), functools.partial(lambda p, k, s, a: (0, a[p, k]), p))
    return pl.pallas_call(
        reorder_kernel,
        grid_spec=pltpu.PrefetchScalarGridSpec(
            num_scalar_prefetch=2,
            grid=(2 * per_half,),
            in_specs=[tile(0), tile(1)],
            out_specs=pl.BlockSpec((rows, TILE), lambda k, s, a: (0, k)),
        ),
        out_shape=jax.ShapeDtypeStruct((rows, 2 * half), own.dtype),
        cost_estimate=pl.CostEstimate(flops=0, bytes_accessed=rows * half, transcendentals=0),
    )(side, at, own, other)


def found(wanted, source, per):
    rel = wanted - source * per
    here = ((rel >= 0) & (rel < per)).astype(jnp.int32)
    return here, jnp.clip(rel, 0, per - 1)


def tile_rows(at):
    return pl.ds(pl.multiple_of(at * TILE, TILE), TILE)


def accumulate_kernel(count, first, blocks, source, here, at, *refs):
    sigmas, pieces = refs[:count], refs[count : 3 * count]
    acc_in, mine_in = (None, None) if first else refs[3 * count : 3 * count + 2]
    acc, mine = refs[-2:]
    j = pl.program_id(0)
    for side in range(2):

        @pl.when(j // blocks == side)
        def _():
            for p in range(count):
                term = jnp.dot(sigmas[p][...], pieces[2 * p + side][...], preferred_element_type=F32)
                if p > 0:
                    acc[...] += term
                elif first:
                    acc[...] = term
                else:
                    acc[...] = acc_in[...] + term
            for t in range(acc.shape[0] // TILE):
                rows = slice(t * TILE, (t + 1) * TILE)
                value = None if first else mine_in[rows, :]
                for p in range(count):
                    q = 2 * p + side
                    got = pieces[q][tile_rows(at[q, t]), :]
                    value = got if value is None else jnp.where(here[q, t] != 0, got, value)
                mine[rows, :] = value


def sides(rows, unit, blocks):
    left = pl.BlockSpec((rows, unit), lambda j, *_: (0, jnp.minimum(j, blocks - 1)))
    right = pl.BlockSpec((rows, unit), lambda j, *_: (0, jnp.maximum(j - blocks, 0)))
    return [left, right]


def accumulate(sigma, sources, pieces, wanted, state, unit):
    count = len(sources)
    sources = [x for pair in sources for x in pair]
    first = state is None
    rows, half = pieces[0][0].shape
    blocks = half // unit
    per = rows // TILE
    marks = [found(wanted, s, per) for s in sources]
    here = jnp.stack([m[0] for m in marks])
    at = jnp.stack([m[1] for m in marks])
    cut = pl.BlockSpec((rows, unit), lambda j, *_: (0, j))
    sigma_specs = [
        pl.BlockSpec((rows, rows), functools.partial(lambda p, j, s, *_: (0, s[2 * p + j // blocks]), p))
        for p in range(count)
    ]
    flat = [x for pair in pieces for x in pair]
    extra = [] if first else list(state)
    start = 3 + 3 * count
    return pl.pallas_call(
        functools.partial(accumulate_kernel, count, first, blocks),
        grid_spec=pltpu.PrefetchScalarGridSpec(
            num_scalar_prefetch=3,
            grid=(2 * blocks,),
            in_specs=sigma_specs + sides(rows, unit, blocks) * count + [cut] * len(extra),
            out_specs=[cut, cut],
        ),
        out_shape=[
            jax.ShapeDtypeStruct((rows, 2 * half), F32),
            jax.ShapeDtypeStruct((rows, 2 * half), flat[0].dtype),
        ],
        input_output_aliases={} if first else {start: 0, start + 1: 1},
        compiler_params=pltpu.CompilerParams(vmem_limit_bytes=VMEM_LIMIT),
        cost_estimate=pl.CostEstimate(flops=count * rows * half, bytes_accessed=rows * half, transcendentals=0),
    )(jnp.stack(sources), here, at, *([sigma] * count), *flat, *extra)


def finish_kernel(blocks, here, at, sigma, left, right, acc, mine, *refs):
    out, part = refs[-2:]
    j = pl.program_id(0)
    for side, late in enumerate((left, right)):

        @pl.when(j // blocks == side)
        def _():
            prod = acc[...] + jnp.dot(sigma[...], late[...], preferred_element_type=F32)
            out[...] = (-prod).astype(out.dtype)
            total = None
            for t in range(acc.shape[0] // TILE):
                rows = slice(t * TILE, (t + 1) * TILE)
                tile = jnp.where(here[t] != 0, late[tile_rows(at[t]), :], mine[rows, :])
                add = tile.astype(F32) * prod[rows]
                total = add if total is None else total + add
            part[...] = jnp.sum(total, axis=0, keepdims=True)


def finish(coeff, source, left, right, state, wanted, unit, begin, out):
    acc, mine = state
    rows, cols = acc.shape
    width = left.shape[1]
    blocks = width // unit
    here, at = found(wanted, source, rows // TILE)
    first, second = begin // unit, (cols // 2 + begin) // unit - blocks
    cut = pl.BlockSpec((rows, unit), lambda j, *_: (0, j + jnp.where(j < blocks, first, second)))
    extra = [] if out is None else [out]
    return pl.pallas_call(
        functools.partial(finish_kernel, blocks),
        grid_spec=pltpu.PrefetchScalarGridSpec(
            num_scalar_prefetch=2,
            grid=(2 * blocks,),
            in_specs=[pl.BlockSpec((rows, rows), lambda j, *_: (0, 0))]
            + sides(rows, unit, blocks)
            + [cut, cut]
            + [pl.BlockSpec(memory_space=pl.ANY)] * len(extra),
            out_specs=[cut, pl.BlockSpec((1, unit), lambda j, *_: (0, j))],
        ),
        out_shape=[
            jax.ShapeDtypeStruct((rows, cols), jnp.bfloat16),
            jax.ShapeDtypeStruct((1, 2 * width), F32),
        ],
        input_output_aliases={} if out is None else {7: 0},
        compiler_params=pltpu.CompilerParams(vmem_limit_bytes=VMEM_LIMIT),
        cost_estimate=pl.CostEstimate(flops=rows * width, bytes_accessed=rows * width, transcendentals=0),
    )(here, at, coeff, left, right, acc, mine, *extra)


def row_sum(value, n):
    step = 1
    if n & (n - 1):
        return lax.psum(value, "row")
    while step < n:
        value = value + lax.ppermute(value, "row", [(i, i ^ step) for i in range(n)])
        step *= 2
    return value


def body(sigma_anc, panel, holder, dinv_diag):
    n = lax.axis_size("row")
    me = lax.axis_index("row")
    rows, cols = panel.shape
    per = rows // TILE
    half = cols // 2
    unit = half // 3 if half % (3 * TILE) == 0 else half
    order = list(range(0, n, 2)) + list(range(1, n, 2))[::-1]
    table = jnp.array(order, jnp.int32)
    place = jnp.array([order.index(i) for i in range(n)], jnp.int32)[me]
    fwd = [(order[i], order[(i + 1) % n]) for i in range(n)]
    bwd = [(b, a) for a, b in fwd]
    ahead = lambda x: lax.ppermute(x, "row", fwd)
    back = lambda x: lax.ppermute(x, "row", bwd)
    wanted = lax.dynamic_slice_in_dim(holder, me * per, per)
    tile_ids = jnp.arange(holder.shape[0], dtype=jnp.int32)
    logical = jnp.sum(
        jnp.where(holder[:, None] == tile_ids[None, :], tile_ids[:, None], 0), axis=0
    )

    own = (panel[:, :half], panel[:, half:])
    (al, ar), (bl, br) = own, own
    state = None
    ready = [((me, me), own)]
    sigma = None
    for hop in range(1, n // 2):
        if hop > 2:
            state = accumulate(sigma, [s for s, _ in ready], [p for _, p in ready], wanted, state, unit)
            ready = []
            al, br, state = lax.optimization_barrier((al, br, state))
        al, br = ahead(al), back(br)
        if hop == 1:
            other = lax.ppermute(sigma_anc, "col", [(0, 1), (1, 0)])
            sigma = reorder(sigma_anc, other, logical)
        if hop == 2:
            ar, bl, sigma = lax.optimization_barrier((ar, bl, sigma))
        ar, bl = ahead(ar), back(bl)
        sources = [table[(place - hop) % n], table[(place + hop) % n]]
        if hop > 1:
            ready += fresh
        fresh = [((sources[0],) * 2, (al, ar)), ((sources[1],) * 2, (bl, br))]
    state = accumulate(sigma, [s for s, _ in ready], [p for _, p in ready], wanted, state, unit)
    al, br, state = lax.optimization_barrier((al, br, state))
    if unit < half:
        wide, thin = half - unit, unit // 2 if unit % (2 * TILE) == 0 else unit
        splits = [(0, wide, unit)] + [(lo, thin, thin) for lo in range(wide, half, thin)]
    else:
        splits = [(0, half, unit)]
    def send(lo, width):
        return ahead(al[:, lo : lo + width]), back(br[:, lo : lo + width])

    late = [send(*splits[0][:2])]
    (from_a, (left, far_right)), (from_b, (far_left, right)) = fresh
    state = accumulate(sigma, [(from_a[0], from_b[0])], [(left, right)], wanted, state, unit)
    al, br, state = lax.optimization_barrier((al, br, state))
    late += [send(lo, w) for lo, w, _ in splits[1:]]
    state = accumulate(sigma, [(from_b[0], from_a[0])], [(far_left, far_right)], wanted, state, unit)
    source = table[(place + n // 2) % n]
    coeff = lax.dynamic_slice_in_dim(sigma, source * rows, rows, axis=1)
    out, parts = None, []
    for (lo, w, step), (left, right) in zip(splits, late):
        out, part = finish(coeff, source, left, right, state, wanted, step, lo, out)
        parts.append((part[:, :w], part[:, w:]))
    part = jnp.concatenate([p for p, _ in parts] + [p for _, p in parts], axis=1)
    return out, dinv_diag + row_sum(part, n).reshape(cols)


def solution(mesh):
    placed = (
        P(("groups", "row"), "col"),
        P(("groups", "row"), "col"),
        P("groups"),
        P(("groups", "col")),
    )
    return jax.shard_map(
        body,
        mesh=mesh,
        in_specs=placed,
        out_specs=(P(("groups", "row"), "col"), P(("groups", "col"))),
        check_vma=False,
    )
```

```python
import functools

import jax
import jax.numpy as jnp
from jax import lax
from jax.experimental import pallas as pl
from jax.experimental.pallas import tpu as pltpu
from jax.sharding import PartitionSpec as P

TILE = 128
F32 = jnp.float32
VMEM_LIMIT = 28 * 1024 * 1024


def reorder_kernel(side, at, own, other, out):
    k = pl.program_id(0)
    out[...] = jnp.where(side[k] == 0, own[...], other[...])


def reorder(own, other, logical):
    rows, half = own.shape
    per_half = half // TILE
    side = (logical // per_half != lax.axis_index("col")).astype(jnp.int32)
    step = jnp.arange(2 * per_half, dtype=jnp.int32)
    upto = step[None, :] <= step[:, None]
    last = lambda flag: jnp.max(jnp.where(upto & flag[None, :], step[None, :], 0), axis=1)
    at = (logical % per_half)[jnp.stack([last(side == 0), last(side == 1)])]
    tile = lambda p: pl.BlockSpec((rows, TILE), functools.partial(lambda p, k, s, a: (0, a[p, k]), p))
    return pl.pallas_call(
        reorder_kernel,
        grid_spec=pltpu.PrefetchScalarGridSpec(
            num_scalar_prefetch=2,
            grid=(2 * per_half,),
            in_specs=[tile(0), tile(1)],
            out_specs=pl.BlockSpec((rows, TILE), lambda k, s, a: (0, k)),
        ),
        out_shape=jax.ShapeDtypeStruct((rows, 2 * half), own.dtype),
        cost_estimate=pl.CostEstimate(flops=0, bytes_accessed=rows * half, transcendentals=0),
    )(side, at, own, other)


def found(wanted, source, per):
    rel = wanted - source * per
    here = ((rel >= 0) & (rel < per)).astype(jnp.int32)
    return here, jnp.clip(rel, 0, per - 1)


def tile_rows(at):
    return pl.ds(pl.multiple_of(at * TILE, TILE), TILE)


def accumulate_kernel(count, first, blocks, source, here, at, *refs):
    sigmas, pieces = refs[:count], refs[count : 3 * count]
    acc_in, mine_in = (None, None) if first else refs[3 * count : 3 * count + 2]
    acc, mine = refs[-2:]
    j = pl.program_id(0)
    for side in range(2):

        @pl.when(j // blocks == side)
        def _():
            for p in range(count):
                term = jnp.dot(sigmas[p][...], pieces[2 * p + side][...], preferred_element_type=F32)
                if p > 0:
                    acc[...] += term
                elif first:
                    acc[...] = term
                else:
                    acc[...] = acc_in[...] + term
            for t in range(acc.shape[0] // TILE):
                rows = slice(t * TILE, (t + 1) * TILE)
                value = None if first else mine_in[rows, :]
                for p in range(count):
                    q = 2 * p + side
                    got = pieces[q][tile_rows(at[q, t]), :]
                    value = got if value is None else jnp.where(here[q, t] != 0, got, value)
                mine[rows, :] = value


def sides(rows, unit, blocks):
    left = pl.BlockSpec((rows, unit), lambda j, *_: (0, jnp.minimum(j, blocks - 1)))
    right = pl.BlockSpec((rows, unit), lambda j, *_: (0, jnp.maximum(j - blocks, 0)))
    return [left, right]


def accumulate(sigma, sources, pieces, wanted, state, unit):
    count = len(sources)
    sources = [x for pair in sources for x in pair]
    first = state is None
    rows, half = pieces[0][0].shape
    blocks = half // unit
    per = rows // TILE
    marks = [found(wanted, s, per) for s in sources]
    here = jnp.stack([m[0] for m in marks])
    at = jnp.stack([m[1] for m in marks])
    cut = pl.BlockSpec((rows, unit), lambda j, *_: (0, j))
    sigma_specs = [
        pl.BlockSpec((rows, rows), functools.partial(lambda p, j, s, *_: (0, s[2 * p + j // blocks]), p))
        for p in range(count)
    ]
    flat = [x for pair in pieces for x in pair]
    extra = [] if first else list(state)
    start = 3 + 3 * count
    return pl.pallas_call(
        functools.partial(accumulate_kernel, count, first, blocks),
        grid_spec=pltpu.PrefetchScalarGridSpec(
            num_scalar_prefetch=3,
            grid=(2 * blocks,),
            in_specs=sigma_specs + sides(rows, unit, blocks) * count + [cut] * len(extra),
            out_specs=[cut, cut],
        ),
        out_shape=[
            jax.ShapeDtypeStruct((rows, 2 * half), F32),
            jax.ShapeDtypeStruct((rows, 2 * half), flat[0].dtype),
        ],
        input_output_aliases={} if first else {start: 0, start + 1: 1},
        compiler_params=pltpu.CompilerParams(vmem_limit_bytes=VMEM_LIMIT),
        cost_estimate=pl.CostEstimate(flops=count * rows * half, bytes_accessed=rows * half, transcendentals=0),
    )(jnp.stack(sources), here, at, *([sigma] * count), *flat, *extra)


def finish_kernel(blocks, here, at, coeff, left, right, acc, mine, *refs):
    *_, out, part, both = refs
    j = pl.program_id(0)
    unit = acc.shape[1]

    if blocks == 1:

        @pl.when(j == 0)
        def _():
            thin = jnp.concatenate([left[...], right[...]], axis=1)
            both[...] = jnp.dot(coeff[...], thin, preferred_element_type=F32)

    for side, late in enumerate((left, right)):

        @pl.when(j // blocks == side)
        def _():
            if blocks == 1:
                term = both[:, side * unit : (side + 1) * unit]
            else:
                term = jnp.dot(coeff[...], late[...], preferred_element_type=F32)
            prod = acc[...] + term
            out[...] = (-prod).astype(out.dtype)
            total = None
            for t in range(acc.shape[0] // TILE):
                rows = slice(t * TILE, (t + 1) * TILE)
                tile = jnp.where(here[t] != 0, late[tile_rows(at[t]), :], mine[rows, :])
                add = tile.astype(F32) * prod[rows]
                total = add if total is None else total + add
            part[...] = jnp.sum(total, axis=0, keepdims=True)


def finish(coeff, source, left, right, state, wanted, unit, begin, out):
    acc, mine = state
    rows, cols = acc.shape
    width = left.shape[1]
    blocks = width // unit
    here, at = found(wanted, source, rows // TILE)
    first, second = begin // unit, (cols // 2 + begin) // unit - blocks
    cut = pl.BlockSpec((rows, unit), lambda j, *_: (0, j + jnp.where(j < blocks, first, second)))
    extra = [] if out is None else [out]
    return pl.pallas_call(
        functools.partial(finish_kernel, blocks),
        grid_spec=pltpu.PrefetchScalarGridSpec(
            num_scalar_prefetch=2,
            grid=(2 * blocks,),
            in_specs=[pl.BlockSpec((rows, rows), lambda j, *_: (0, 0))]
            + sides(rows, unit, blocks)
            + [cut, cut]
            + [pl.BlockSpec(memory_space=pl.ANY)] * len(extra),
            out_specs=[cut, pl.BlockSpec((1, unit), lambda j, *_: (0, j))],
            scratch_shapes=[pltpu.VMEM((rows, 2 * unit) if blocks == 1 else (8, TILE), F32)],
        ),
        out_shape=[
            jax.ShapeDtypeStruct((rows, cols), jnp.bfloat16),
            jax.ShapeDtypeStruct((1, 2 * width), F32),
        ],
        input_output_aliases={} if out is None else {7: 0},
        compiler_params=pltpu.CompilerParams(vmem_limit_bytes=VMEM_LIMIT),
        cost_estimate=pl.CostEstimate(flops=rows * width, bytes_accessed=rows * width, transcendentals=0),
    )(here, at, coeff, left, right, acc, mine, *extra)


def row_sum(value, n):
    step = 1
    if n & (n - 1):
        return lax.psum(value, "row")
    while step < n:
        value = value + lax.ppermute(value, "row", [(i, i ^ step) for i in range(n)])
        step *= 2
    return value


def body(sigma_anc, panel, holder, dinv_diag):
    n = lax.axis_size("row")
    me = lax.axis_index("row")
    rows, cols = panel.shape
    per = rows // TILE
    half = cols // 2
    unit = half // 3 if half % (3 * TILE) == 0 else half
    order = list(range(0, n, 2)) + list(range(1, n, 2))[::-1]
    table = jnp.array(order, jnp.int32)
    place = jnp.array([order.index(i) for i in range(n)], jnp.int32)[me]
    fwd = [(order[i], order[(i + 1) % n]) for i in range(n)]
    bwd = [(b, a) for a, b in fwd]
    ahead = lambda x: lax.ppermute(x, "row", fwd)
    back = lambda x: lax.ppermute(x, "row", bwd)
    wanted = lax.dynamic_slice_in_dim(holder, me * per, per)
    tile_ids = jnp.arange(holder.shape[0], dtype=jnp.int32)
    logical = jnp.sum(
        jnp.where(holder[:, None] == tile_ids[None, :], tile_ids[:, None], 0), axis=0
    )

    own = (panel[:, :half], panel[:, half:])
    (al, ar), (bl, br) = own, own
    state = None
    ready = [((me, me), own)]
    sigma = None
    for hop in range(1, n // 2):
        if hop > 2:
            state = accumulate(sigma, [s for s, _ in ready], [p for _, p in ready], wanted, state, unit)
            ready = []
            al, br, state = lax.optimization_barrier((al, br, state))
        al, br = ahead(al), back(br)
        if hop == 1:
            other = lax.ppermute(sigma_anc, "col", [(0, 1), (1, 0)])
            sigma = reorder(sigma_anc, other, logical)
        if hop == 2:
            ar, bl, sigma = lax.optimization_barrier((ar, bl, sigma))
        ar, bl = ahead(ar), back(bl)
        sources = [table[(place - hop) % n], table[(place + hop) % n]]
        if hop > 1:
            ready += fresh
        fresh = [((sources[0],) * 2, (al, ar)), ((sources[1],) * 2, (bl, br))]
    state = accumulate(sigma, [s for s, _ in ready], [p for _, p in ready], wanted, state, unit)
    al, br, state = lax.optimization_barrier((al, br, state))
    if unit < half:
        wide, thin = half - unit, unit // 2 if unit % (2 * TILE) == 0 else unit
        splits = [(0, wide, unit)] + [(lo, thin, thin) for lo in range(wide, half, thin)]
    else:
        splits = [(0, half, unit)]
    def send(lo, width):
        return ahead(al[:, lo : lo + width]), back(br[:, lo : lo + width])

    late = [send(*splits[0][:2])]
    (from_a, (left, far_right)), (from_b, (far_left, right)) = fresh
    state = accumulate(sigma, [(from_a[0], from_b[0])], [(left, right)], wanted, state, unit)
    al, br, state = lax.optimization_barrier((al, br, state))
    late += [send(lo, w) for lo, w, _ in splits[1:]]
    state = accumulate(sigma, [(from_b[0], from_a[0])], [(far_left, far_right)], wanted, state, unit)
    source = table[(place + n // 2) % n]
    coeff = lax.dynamic_slice_in_dim(sigma, source * rows, rows, axis=1)
    out, parts = None, []
    for (lo, w, step), (left, right) in zip(splits, late):
        out, part = finish(coeff, source, left, right, state, wanted, step, lo, out)
        parts.append((part[:, :w], part[:, w:]))
    part = jnp.concatenate([p for p, _ in parts] + [p for _, p in parts], axis=1)
    return out, dinv_diag + row_sum(part, n).reshape(cols)


def solution(mesh):
    placed = (
        P(("groups", "row"), "col"),
        P(("groups", "row"), "col"),
        P("groups"),
        P(("groups", "col")),
    )
    return jax.shard_map(
        body,
        mesh=mesh,
        in_specs=placed,
        out_specs=(P(("groups", "row"), "col"), P(("groups", "col"))),
        check_vma=False,
    )
```
